128 devices in a mesh: replica: 16 (over y, z), tensor: 8 (over x, core).
Axes of the slice: x: 4, y: 4, z: 4, core: 2. Of those that a mesh axis runs over, the one named last changes fastest.
Arguments:
- inner_change: bfloat16 [32768, 14336], P('replica', 'tensor'), may hold values from -6 to 6
- error_memory: bfloat16 [32768, 14336], P('replica', 'tensor'), may hold values from -4 to 4
- momentum: float32 [4096, 14336], P('replica', 'tensor'), may hold values from -2 to 2
- q_prev: float32 [32, 14336], P(None, 'tensor'), may hold values from -6 to 6
Outputs:
- outer_update: bfloat16 [4096, 14336], P('replica', 'tensor')
- new_momentum: float32 [4096, 14336], P('replica', 'tensor')
- new_error: bfloat16 [32768, 14336], P('replica', 'tensor')
- new_q: float32 [32, 14336], P(None, 'tensor')
The draws below stay inside these ranges and needn't reach their ends.
All inputs are finite; a program needn't handle non-finite values.
Results may differ from the reference program's by a relative error of at most 0.003.
Values sent between devices are 32-bit elements; how exact they have to be, the bound alone decides.
No kernel may reach another device: no remote copies, remote signals or barrier semaphores. Data moves between devices by JAX's collectives and lax.ppermute only.
A program may use at most 128 MiB of HBM per device.

```python
import jax
import jax.numpy as jnp
from jax import lax

ROWS = 4096
FF = 14336
RANK = 32
REPLICAS = 8


def block_levels(key, shape, split, low, top_value):
    def one(position, parts):
        draws = jax.random.uniform(jax.random.fold_in(jax.random.fold_in(key, 6), position), (parts,), jnp.float32, low / len(split), top_value / len(split))
        return jnp.repeat(jnp.exp(draws), shape[position] // parts).reshape((-1,) + (1,) * (len(shape) - position - 1))

    loudness = one(*split[0])
    for cut in split[1:]:
        loudness = loudness * one(*cut)
    return loudness


def scatter_about(rng, shape, scale, most, cuts=(), dtype=jnp.bfloat16):
    values = scale * jax.random.normal(rng, shape, jnp.float32)
    if cuts:
        values = values * block_levels(rng, shape, cuts, -0.22, 0.18)
    return jnp.clip(values, -most, most).astype(dtype)


def setup_inputs(seed: int = 0) -> dict:
    keys = jax.random.split(jax.random.key(seed), 5)
    return {
        "inner_change": scatter_about(keys[0], (REPLICAS * ROWS, FF), 1.0, 6.0, ((0, 16), (1, 8))),
        "error_memory": scatter_about(keys[1], (REPLICAS * ROWS, FF), 0.5, 4.0, ((0, 16), (1, 8))),
        "momentum": scatter_about(keys[2], (ROWS, FF), 0.3, 2.0, ((0, 16), (1, 8)), jnp.float32),
        "q_prev": scatter_about(keys[3], (RANK, FF), 1.0, 6.0, ((1, 8),), jnp.float32),
    }


def reference(inner_change, error_memory, momentum, q_prev):
    high = lax.Precision.HIGHEST
    inner_blocks = inner_change.reshape(REPLICAS, ROWS, FF)
    error_blocks = error_memory.reshape(REPLICAS, ROWS, FF)

    def accumulate(total, pair):
        return (total + (pair[1].astype(jnp.float32) - pair[0].astype(jnp.float32)), None)
    total, _ = lax.scan(accumulate, jnp.zeros((ROWS, FF), jnp.float32), (inner_blocks, error_blocks))
    p_sum = jnp.dot(q_prev.astype(jnp.float32), total.T.astype(jnp.float32), precision=high, preferred_element_type=jnp.float32)
    gram = jnp.dot(p_sum.astype(jnp.float32), p_sum.T.astype(jnp.float32), precision=high, preferred_element_type=jnp.float32)
    chol = jnp.linalg.cholesky(gram)
    basis = jax.scipy.linalg.solve_triangular(chol, p_sum, lower=True)
    new_q = jnp.dot(basis.astype(jnp.float32), total.astype(jnp.float32), precision=high, preferred_element_type=jnp.float32) / REPLICAS
    approx = jnp.dot(basis.T.astype(jnp.float32), new_q.astype(jnp.float32), precision=high, preferred_element_type=jnp.float32)

    def residue(pair):
        return (pair[1].astype(jnp.float32) - pair[0].astype(jnp.float32) - approx).astype(jnp.bfloat16)
    new_error = lax.map(residue, (inner_blocks, error_blocks)).reshape(REPLICAS * ROWS, FF)
    new_momentum = 0.9 * momentum + approx
    outer_update = (0.7 * (approx + 0.9 * new_momentum)).astype(jnp.bfloat16)
    return (outer_update, new_momentum, new_error, new_q)
```

```python
import jax
import jax.numpy as jnp
from jax import lax
from jax.experimental import pallas as pl
from jax.experimental.pallas import tpu as pltpu
from jax.sharding import PartitionSpec as P

RING = 4
BOTH = ("replica", "tensor")
RANK = 32
CHUNK = 256
STATE = 256
HBM = pl.BlockSpec(memory_space=pltpu.HBM)
VMEM = pl.BlockSpec(memory_space=pltpu.VMEM)


def swap_pairs(even, odd):
    pairs = []
    for device in range(RING**3 * 2):
        place = {
            "c": device % 2,
            "x": device // 2 % RING,
            "z": device // (2 * RING) % RING,
            "y": device // (2 * RING * RING),
        }
        axis, flip = (even, odd)[place["c"]]
        place[axis] ^= flip
        target = ((place["y"] * RING + place["z"]) * RING + place["x"]) * 2 + place["c"]
        pairs.append((device, target))
    return pairs


def swap(value, even, odd=None):
    return lax.ppermute(value, BOTH, swap_pairs(even, odd or even))


def sum_four(value, even, odd):
    one, two, three = (swap(value, (even, k), (odd, k)) for k in (1, 2, 3))
    return (value + one) + (two + three)


def split(value, count):
    parts = []
    for _ in range(count):
        part = value.astype(jnp.bfloat16)
        parts.append(part)
        value = value - part.astype(jnp.float32)
    return parts


def fold(value):
    return (value[:RANK] + value[RANK : 2 * RANK]) + value[2 * RANK : 3 * RANK]


NT = (((1,), (1,)), ((), ()))


def params(mebibytes):
    return pltpu.CompilerParams(vmem_limit_bytes=mebibytes * 1024 * 1024)


def core_of():
    return lax.rem(lax.axis_index("tensor"), 2)


def left_kernel(q_ref, error_hbm, change_hbm, send_ref, keep_ref, error_ref, change_ref, factor_ref, sems):
    core = core_of()
    half = send_ref.shape[1]
    count = 2 * half // CHUNK
    blocks, copies = [], []
    for k in range(count):
        side = (1 - core) if k < count // 2 else core
        rows = pl.ds(pl.multiple_of(side * half + k % (count // 2) * CHUNK, CHUNK), CHUNK)
        pair = [
            pltpu.make_async_copy(source.at[rows], target.at[rows], sems.at[j, k])
            for j, (source, target) in enumerate(((error_hbm, error_ref), (change_hbm, change_ref)))
        ]
        for copy in pair:
            copy.start()
        blocks.append(rows)
        copies.append(pair)
    parts = [part.astype(jnp.float32) for part in split(q_ref[...], 3)]
    stacked = jnp.concatenate(parts + [jnp.zeros_like(parts[0])], axis=0)
    factor_ref[...] = stacked.T.astype(jnp.bfloat16)
    for k in range(count):
        for copy in copies[k]:
            copy.wait()
        term = jnp.dot(error_ref[blocks[k], :], factor_ref[...], preferred_element_type=jnp.float32)
        term -= jnp.dot(change_ref[blocks[k], :], factor_ref[...], preferred_element_type=jnp.float32)
        target = send_ref if k < count // 2 else keep_ref
        start = k % (count // 2) * CHUNK
        target[:, start : start + CHUNK] = fold(term.T)


def left_factor(q_prev, error_memory, inner_change):
    rows, columns = error_memory.shape
    half = rows // 2
    return pl.pallas_call(
        left_kernel,
        in_specs=[VMEM, HBM, HBM],
        out_specs=[VMEM] * 4,
        out_shape=[
            pltpu.VMEM((RANK, half), jnp.float32),
            pltpu.VMEM((RANK, half), jnp.float32),
            pltpu.VMEM((rows, columns), jnp.bfloat16),
            pltpu.VMEM((rows, columns), jnp.bfloat16),
        ],
        scratch_shapes=[
            pltpu.VMEM((columns, 4 * RANK), jnp.bfloat16),
            pltpu.SemaphoreType.DMA((2, rows // CHUNK)),
        ],
        compiler_params=params(8),
        cost_estimate=pl.CostEstimate(
            flops=12 * RANK * rows * columns, bytes_accessed=4 * rows * columns, transcendentals=0
        ),
        name="left_factor",
    )(q_prev, pltpu.with_memory_space_constraint(error_memory, pltpu.HBM),
      pltpu.with_memory_space_constraint(inner_change, pltpu.HBM))


def right_products(left_ref, error_ref, change_ref, side, previous_ref, out_ref):
    half, columns = left_ref.shape[1], error_ref.shape[1]
    rows = pl.ds(pl.multiple_of(side * half, half), half)
    factor = jnp.concatenate(split(left_ref[...], 3), axis=0)
    for start in range(0, columns, CHUNK):
        block = slice(start, start + CHUNK)
        term = jnp.dot(factor, error_ref[rows, block], preferred_element_type=jnp.float32)
        term -= jnp.dot(factor, change_ref[rows, block], preferred_element_type=jnp.float32)
        value = fold(term)
        if previous_ref is not None:
            value = value + previous_ref[:, block]
        out_ref[:, block] = value
    squares = fold(lax.dot_general(factor, factor, NT, preferred_element_type=jnp.float32))
    return (squares[:, :RANK] + squares[:, RANK : 2 * RANK]) + squares[:, 2 * RANK :]


def first_kernel(own_ref, error_ref, change_ref, out_ref, gram_ref):
    gram = right_products(own_ref, error_ref, change_ref, core_of(), None, out_ref)
    gram_ref[...] = jnp.concatenate([gram, jnp.zeros((RANK, 128 - RANK), jnp.float32)], axis=1)


def second_kernel(own_ref, other_ref, error_ref, change_ref, previous_ref, gram_ref, out_ref, whole_ref, share_ref):
    core = core_of()
    half = own_ref.shape[1]
    gram = right_products(other_ref, error_ref, change_ref, 1 - core, previous_ref, out_ref)
    share_ref[:, :128] = gram_ref[...] + jnp.concatenate(
        [gram, jnp.zeros((RANK, 128 - RANK), jnp.float32)], axis=1
    )
    whole_ref[:, pl.ds(pl.multiple_of(core * half, half), half)] = own_ref[...]
    whole_ref[:, pl.ds(pl.multiple_of((1 - core) * half, half), half)] = other_ref[...]
    position = lax.axis_index("replica")
    neighbour = position + 1 - 2 * lax.rem(position, 2)
    start = lax.rem(neighbour, 8) * STATE
    share_ref[:, 128:] = whole_ref[:, pl.ds(pl.multiple_of(start, STATE), STATE)]


def right_factor(own, other, error, change):
    rows, columns = error.shape
    half = own.shape[1]
    cost = pl.CostEstimate(
        flops=12 * RANK * half * columns, bytes_accessed=4 * half * columns, transcendentals=0
    )
    projected, gram = pl.pallas_call(
        first_kernel,
        in_specs=[VMEM] * 3,
        out_specs=[VMEM] * 2,
        out_shape=[
            pltpu.VMEM((RANK, columns), jnp.float32),
            pltpu.VMEM((RANK, 128), jnp.float32),
        ],
        compiler_params=params(8),
        cost_estimate=cost,
        name="right_first",
    )(own, error, change)
    return pl.pallas_call(
        second_kernel,
        in_specs=[VMEM] * 6,
        out_specs=[VMEM] * 3,
        out_shape=[
            pltpu.VMEM((RANK, columns), jnp.float32),
            pltpu.VMEM((RANK, rows), jnp.float32),
            pltpu.VMEM((RANK, 128 + STATE), jnp.float32),
        ],
        compiler_params=params(8),
        cost_estimate=cost,
        name="right_second",
    )(own, other, error, change, projected, gram)


def basis_kernel(whole_ref, mine_ref, theirs_ref, inverse_ref, basis_ref):
    width = 128
    row = lax.broadcasted_iota(jnp.int32, (RANK, width), 0)
    column = lax.broadcasted_iota(jnp.int32, (RANK, width), 1)
    gram = mine_ref[:, :width] + theirs_ref[:, :width]
    work = jnp.where(column < RANK, gram, jnp.where(column - RANK == row, 1.0, 0.0))
    for j in range(RANK):
        pivot = work[j : j + 1, :]
        scale = lax.rsqrt(pivot[:, j : j + 1])
        scaled = pivot * scale
        factor = work[:, j : j + 1] * scale
        work = jnp.where(row > j, work - factor * scaled, jnp.where(row == j, scaled, work))
    inverse = work[:, RANK : 2 * RANK]
    inverse_ref[...] = jnp.concatenate([inverse, jnp.zeros((RANK, width - RANK), jnp.float32)], axis=1)
    rows = whole_ref.shape[1]
    position = lax.axis_index("replica")
    start = lax.rem(position, 8) * STATE
    mine = whole_ref[:, pl.ds(pl.multiple_of(start, STATE), STATE)]
    state = jnp.where(lax.rem(position, 2) == position // 8, mine, theirs_ref[:, width:])
    for offset, count, value in ((0, rows, whole_ref[...]), (rows, STATE, state)):
        basis = jnp.dot(inverse, value, precision=lax.Precision.HIGHEST, preferred_element_type=jnp.float32)
        top, low = (part.astype(jnp.float32) for part in split(basis, 2))
        stacked = jnp.concatenate([top, low, top, low], axis=0)
        basis_ref[offset : offset + count, :] = stacked.T.astype(jnp.bfloat16)


def make_basis(whole, mine, theirs):
    rows = whole.shape[1]
    return pl.pallas_call(
        basis_kernel,
        in_specs=[VMEM] * 3,
        out_specs=[VMEM, VMEM],
        out_shape=[
            pltpu.VMEM((RANK, 128), jnp.float32),
            pltpu.VMEM((rows + STATE, 128), jnp.bfloat16),
        ],
        compiler_params=params(8),
        cost_estimate=pl.CostEstimate(
            flops=24 * RANK * RANK * rows, bytes_accessed=16 * RANK * rows, transcendentals=0
        ),
        name="basis",
    )(whole, mine, theirs)


def apply_kernel(
    count, summed_ref, inverse_ref, basis_ref, error_ref, change_ref, momentum_ref,
    update_hbm, momentum_hbm, error_hbm, q_ref,
    momentum_out_ref, update_ref, error_out_ref, sems,
):
    rows, columns = error_ref.shape
    new_q = (
        jnp.dot(
            inverse_ref[:, :RANK], summed_ref[...],
            precision=lax.Precision.HIGHEST, preferred_element_type=jnp.float32,
        )
        / count
    )
    q_ref[...] = new_q
    top, low = split(new_q, 2)
    factor = jnp.concatenate([top, top, low, low], axis=0)
    started = []
    for k in range(rows // CHUNK):
        block = pl.ds(k * CHUNK, CHUNK)
        approx = jnp.dot(basis_ref[block, :], factor, preferred_element_type=jnp.float32)
        combined = error_ref[block, :].astype(jnp.float32) - change_ref[block, :].astype(jnp.float32)
        error_out_ref[block, :] = (combined - approx).astype(jnp.bfloat16)
        copy = pltpu.make_async_copy(error_out_ref.at[block], error_hbm.at[block], sems.at[2 + k])
        copy.start()
        started.append(copy)
    approx = jnp.dot(basis_ref[pl.ds(rows, STATE), :], factor, preferred_element_type=jnp.float32)
    momentum = 0.9 * momentum_ref[...] + approx
    momentum_out_ref[...] = momentum
    update_ref[...] = (0.7 * (approx + 0.9 * momentum)).astype(jnp.bfloat16)
    for copy in (
        pltpu.make_async_copy(momentum_out_ref, momentum_hbm, sems.at[0]),
        pltpu.make_async_copy(update_ref, update_hbm, sems.at[1]),
    ):
        copy.start()
        started.append(copy)
    for copy in started:
        copy.wait()


def apply_factors(count, summed, inverse, basis, error, change, momentum):
    rows, columns = error.shape
    state = momentum.shape
    return pl.pallas_call(
        lambda *refs: apply_kernel(count, *refs),
        in_specs=[VMEM] * 6,
        out_specs=[HBM, HBM, HBM, VMEM],
        out_shape=[
            pltpu.HBM(state, jnp.bfloat16),
            pltpu.HBM(state, jnp.float32),
            pltpu.HBM((rows, columns), jnp.bfloat16),
            jax.ShapeDtypeStruct((RANK, columns), jnp.float32),
        ],
        scratch_shapes=[
            pltpu.VMEM(state, jnp.float32),
            pltpu.VMEM(state, jnp.bfloat16),
            pltpu.VMEM((rows, columns), jnp.bfloat16),
            pltpu.SemaphoreType.DMA((2 + rows // CHUNK,)),
        ],
        compiler_params=params(18),
        cost_estimate=pl.CostEstimate(
            flops=8 * RANK * rows * columns, bytes_accessed=6 * rows * columns, transcendentals=0
        ),
        name="apply",
    )(summed, inverse, basis, error, change, momentum)


def shards(inner_change, error_memory, momentum, q_prev):
    replicas = lax.axis_size("replica") // 2

    send, keep, error, change = left_factor(q_prev, error_memory, inner_change)
    own = keep + swap(send, ("c", 1))
    own = sum_four(own, "x", "y")
    own = sum_four(own, "y", "x")
    own = own + swap(own, ("z", 2))
    other = swap(own, ("c", 1))

    projected, whole, mine = right_factor(own, other, error, change)
    theirs = swap(mine, ("z", 1))
    summed = sum_four(projected, "y", "z")
    summed, theirs = lax.optimization_barrier((summed, theirs))
    inverse, basis = make_basis(whole, mine, theirs)
    summed = sum_four(summed, "z", "y")
    update, new_momentum, new_error, new_q = apply_factors(
        replicas, summed, inverse, basis, error, change, momentum
    )
    return (update, new_momentum, new_error, new_q)


def solution(mesh):
    in_specs = (
        P("replica", "tensor"),
        P("replica", "tensor"),
        P("replica", "tensor"),
        P(None, "tensor"),
    )
    out_specs = (
        P("replica", "tensor"),
        P("replica", "tensor"),
        P("replica", "tensor"),
        P(None, "tensor"),
    )
    return jax.shard_map(shards, mesh=mesh, in_specs=in_specs, out_specs=out_specs, check_vma=False)
```

```python
import jax
import jax.numpy as jnp
from jax import lax
from jax.experimental import pallas as pl
from jax.experimental.pallas import tpu as pltpu
from jax.sharding import PartitionSpec as P

RING = 4
BOTH = ("replica", "tensor")
RANK = 32
LEFT_CHUNK = 512
CHUNK = 256
STATE = 256
HBM = pl.BlockSpec(memory_space=pltpu.HBM)
VMEM = pl.BlockSpec(memory_space=pltpu.VMEM)


def role_of(x, y, core):
    return (core + x // 2 + y // 2) % 2


def pairs_of(specs, by_role):
    pairs = []
    for device in range(RING**3 * 2):
        core, x = device % 2, device // 2 % RING
        z, y = device // (2 * RING) % RING, device // (2 * RING * RING)
        kind = role_of(x, y, core) if by_role else core
        axis, flip = specs[kind]
        if axis == "c":
            core ^= flip
        else:
            x, y, z = x ^ (flip * (axis == "x")), y ^ (flip * (axis == "y")), z ^ (flip * (axis == "z"))
            if by_role:
                core = role_of(x, y, kind)
        pairs.append((device, ((y * RING + z) * RING + x) * 2 + core))
    return pairs


def swap(value, even, odd=None, by_role=False):
    return lax.ppermute(value, BOTH, pairs_of((even, odd or even), by_role))


def sum_four(value, even, odd, order, by_role=False):
    parts = {k: swap(value, (even, k), (odd, k), by_role) for k in order}
    return (value + parts[1]) + (parts[2] + parts[3])


def split(value, count):
    parts = []
    for _ in range(count):
        part = value.astype(jnp.bfloat16)
        parts.append(part)
        value = value - part.astype(jnp.float32)
    return parts


def fold(value):
    return (value[:RANK] + value[RANK : 2 * RANK]) + value[2 * RANK : 3 * RANK]


NT = (((1,), (1,)), ((), ()))


def params(mebibytes):
    return pltpu.CompilerParams(vmem_limit_bytes=mebibytes * 1024 * 1024)


def own_role():
    tensor, replica = lax.axis_index("tensor"), lax.axis_index("replica")
    return lax.rem(lax.rem(tensor, 2) + tensor // 4 + replica // 8, 2)


def left_terms(factor_ref, error_ref, change_ref, rows):
    term = jnp.dot(error_ref[rows, :], factor_ref[...], preferred_element_type=jnp.float32)
    term -= jnp.dot(change_ref[rows, :], factor_ref[...], preferred_element_type=jnp.float32)
    return fold(term.T)


def left_kernel(
    q_hbm, error_hbm, change_hbm, send_ref, keep_ref, factor_ref, error_ref, change_ref, q_ref, q_sem, sems
):
    role = own_role()
    half = send_ref.shape[1]
    count = 2 * half // LEFT_CHUNK
    fetch = pltpu.make_async_copy(q_hbm, q_ref, q_sem)
    fetch.start()
    blocks, copies = [], []
    for k in range(count):
        side = (1 - role) if k < count // 2 else role
        start = pl.multiple_of(side * half + k % (count // 2) * LEFT_CHUNK, LEFT_CHUNK)
        rows = pl.ds(start, LEFT_CHUNK)
        blocks.append(rows)
        copies.append([
            pltpu.make_async_copy(source.at[rows], target.at[rows], sems.at[j, k])
            for j, (source, target) in enumerate(((error_hbm, error_ref), (change_hbm, change_ref)))
        ])

    def begin(k):
        if k < count:
            for copy in copies[k]:
                copy.start()

    begin(0)
    fetch.wait()
    begin(1)
    parts = [part.astype(jnp.float32) for part in split(q_ref[...], 3)]
    stacked = jnp.concatenate(parts + [jnp.zeros_like(parts[0])], axis=0)
    factor_ref[...] = stacked.T.astype(jnp.bfloat16)
    for k in range(count):
        for copy in copies[k]:
            copy.wait()
        begin(k + 2)
        if k < count // 2:
            send_ref[:, k * LEFT_CHUNK : (k + 1) * LEFT_CHUNK] = left_terms(
                factor_ref, error_ref, change_ref, blocks[k]
            )
        elif k < count - 1:
            start = (k - count // 2) * LEFT_CHUNK
            keep_ref[:, start : start + LEFT_CHUNK] = left_terms(factor_ref, error_ref, change_ref, blocks[k])


def rest_kernel(factor_ref, error_ref, change_ref, keep_ref, out_ref):
    half = out_ref.shape[1]
    done = half - LEFT_CHUNK
    out_ref[:, :done] = keep_ref[...]
    rows = pl.ds(pl.multiple_of(own_role() * half + done, LEFT_CHUNK), LEFT_CHUNK)
    out_ref[:, done:] = left_terms(factor_ref, error_ref, change_ref, rows)


def left_factor(q_prev, error_memory, inner_change):
    rows, columns = error_memory.shape
    half = rows // 2
    send, keep, factor, error, change = pl.pallas_call(
        left_kernel,
        in_specs=[HBM, HBM, HBM],
        out_specs=[VMEM] * 5,
        out_shape=[
            pltpu.VMEM((RANK, half), jnp.float32),
            pltpu.VMEM((RANK, half - LEFT_CHUNK), jnp.float32),
            pltpu.VMEM((columns, 4 * RANK), jnp.bfloat16),
            pltpu.VMEM((rows, columns), jnp.bfloat16),
            pltpu.VMEM((rows, columns), jnp.bfloat16),
        ],
        scratch_shapes=[
            pltpu.VMEM((RANK, columns), jnp.float32),
            pltpu.SemaphoreType.DMA,
            pltpu.SemaphoreType.DMA((2, rows // LEFT_CHUNK)),
        ],
        compiler_params=params(8),
        cost_estimate=pl.CostEstimate(
            flops=12 * RANK * rows * columns, bytes_accessed=4 * rows * columns, transcendentals=0
        ),
        name="left_factor",
    )(*(pltpu.with_memory_space_constraint(value, pltpu.HBM) for value in (q_prev, error_memory, inner_change)))
    keep = pl.pallas_call(
        rest_kernel,
        in_specs=[VMEM] * 4,
        out_specs=VMEM,
        out_shape=pltpu.VMEM((RANK, half), jnp.float32),
        compiler_params=params(8),
        cost_estimate=pl.CostEstimate(
            flops=12 * RANK * LEFT_CHUNK * columns,
            bytes_accessed=4 * LEFT_CHUNK * columns,
            transcendentals=0,
        ),
        name="left_rest",
    )(factor, error, change, keep)
    return send, keep, error, change


def right_products(left_ref, error_ref, change_ref, side, previous_ref, out_ref):
    half, columns = left_ref.shape[1], error_ref.shape[1]
    rows = pl.ds(pl.multiple_of(side * half, half), half)
    factor = jnp.concatenate(split(left_ref[...], 3), axis=0)
    for start in range(0, columns, CHUNK):
        block = slice(start, start + CHUNK)
        term = jnp.dot(factor, error_ref[rows, block], preferred_element_type=jnp.float32)
        term -= jnp.dot(factor, change_ref[rows, block], preferred_element_type=jnp.float32)
        value = fold(term)
        if previous_ref is not None:
            value = value + previous_ref[:, block]
        out_ref[:, block] = value
    squares = fold(lax.dot_general(factor, factor, NT, preferred_element_type=jnp.float32))
    return (squares[:, :RANK] + squares[:, RANK : 2 * RANK]) + squares[:, 2 * RANK :]


def first_kernel(own_ref, error_ref, change_ref, out_ref, gram_ref):
    gram = right_products(own_ref, error_ref, change_ref, own_role(), None, out_ref)
    gram_ref[...] = jnp.concatenate([gram, jnp.zeros((RANK, 128 - RANK), jnp.float32)], axis=1)


def second_kernel(own_ref, other_ref, error_ref, change_ref, previous_ref, gram_ref, out_ref, whole_ref, share_ref):
    role = own_role()
    half = own_ref.shape[1]
    gram = right_products(other_ref, error_ref, change_ref, 1 - role, previous_ref, out_ref)
    share_ref[:, :128] = gram_ref[...] + jnp.concatenate(
        [gram, jnp.zeros((RANK, 128 - RANK), jnp.float32)], axis=1
    )
    whole_ref[:, pl.ds(pl.multiple_of(role * half, half), half)] = own_ref[...]
    whole_ref[:, pl.ds(pl.multiple_of((1 - role) * half, half), half)] = other_ref[...]
    position = lax.axis_index("replica")
    neighbour = position + 1 - 2 * lax.rem(position, 2)
    start = lax.rem(neighbour, 8) * STATE
    share_ref[:, 128:] = whole_ref[:, pl.ds(pl.multiple_of(start, STATE), STATE)]


def right_factor(own, other, error, change):
    rows, columns = error.shape
    half = own.shape[1]
    cost = pl.CostEstimate(
        flops=12 * RANK * half * columns, bytes_accessed=4 * half * columns, transcendentals=0
    )
    projected, gram = pl.pallas_call(
        first_kernel,
        in_specs=[VMEM] * 3,
        out_specs=[VMEM] * 2,
        out_shape=[
            pltpu.VMEM((RANK, columns), jnp.float32),
            pltpu.VMEM((RANK, 128), jnp.float32),
        ],
        compiler_params=params(8),
        cost_estimate=cost,
        name="right_first",
    )(own, error, change)
    return pl.pallas_call(
        second_kernel,
        in_specs=[VMEM] * 6,
        out_specs=[VMEM] * 3,
        out_shape=[
            pltpu.VMEM((RANK, columns), jnp.float32),
            pltpu.VMEM((RANK, rows), jnp.float32),
            pltpu.VMEM((RANK, 128 + STATE), jnp.float32),
        ],
        compiler_params=params(8),
        cost_estimate=cost,
        name="right_second",
    )(own, other, error, change, projected, gram)


def basis_kernel(whole_ref, mine_ref, theirs_ref, inverse_ref, basis_ref):
    width = 128
    row = lax.broadcasted_iota(jnp.int32, (RANK, width), 0)
    column = lax.broadcasted_iota(jnp.int32, (RANK, width), 1)
    gram = mine_ref[:, :width] + theirs_ref[:, :width]
    work = jnp.where(column < RANK, gram, jnp.where(column - RANK == row, 1.0, 0.0))
    for j in range(RANK):
        pivot = work[j : j + 1, :]
        scale = lax.rsqrt(pivot[:, j : j + 1])
        scaled = pivot * scale
        factor = work[:, j : j + 1] * scale
        work = jnp.where(row > j, work - factor * scaled, jnp.where(row == j, scaled, work))
    inverse = work[:, RANK : 2 * RANK]
    inverse_ref[...] = jnp.concatenate([inverse, jnp.zeros((RANK, width - RANK), jnp.float32)], axis=1)
    rows = whole_ref.shape[1]
    position = lax.axis_index("replica")
    start = lax.rem(position, 8) * STATE
    mine = whole_ref[:, pl.ds(pl.multiple_of(start, STATE), STATE)]
    state = jnp.where(lax.rem(position, 2) == position // 8, mine, theirs_ref[:, width:])
    for offset, count, value in ((0, rows, whole_ref[...]), (rows, STATE, state)):
        basis = jnp.dot(inverse, value, precision=lax.Precision.HIGHEST, preferred_element_type=jnp.float32)
        top, low = (part.astype(jnp.float32) for part in split(basis, 2))
        stacked = jnp.concatenate([top, low, top, low], axis=0)
        basis_ref[offset : offset + count, :] = stacked.T.astype(jnp.bfloat16)


def make_basis(whole, mine, theirs):
    rows = whole.shape[1]
    return pl.pallas_call(
        basis_kernel,
        in_specs=[VMEM] * 3,
        out_specs=[VMEM, VMEM],
        out_shape=[
            pltpu.VMEM((RANK, 128), jnp.float32),
            pltpu.VMEM((rows + STATE, 128), jnp.bfloat16),
        ],
        compiler_params=params(8),
        cost_estimate=pl.CostEstimate(
            flops=24 * RANK * RANK * rows, bytes_accessed=16 * RANK * rows, transcendentals=0
        ),
        name="basis",
    )(whole, mine, theirs)


def apply_kernel(
    count, summed_ref, inverse_ref, basis_ref, error_ref, change_ref, momentum_ref,
    update_hbm, momentum_hbm, error_hbm, q_ref,
    momentum_out_ref, update_ref, error_out_ref, sems,
):
    rows, columns = error_ref.shape
    new_q = (
        jnp.dot(
            inverse_ref[:, :RANK], summed_ref[...],
            precision=lax.Precision.HIGHEST, preferred_element_type=jnp.float32,
        )
        / count
    )
    q_ref[...] = new_q
    top, low = split(new_q, 2)
    factor = jnp.concatenate([top, top, low, low], axis=0)
    started = []
    starts = [0, CHUNK // 2, *range(CHUNK, rows, CHUNK), rows]
    for k, (start, end) in enumerate(zip(starts, starts[1:])):
        block = pl.ds(start, end - start)
        approx = jnp.dot(basis_ref[block, :], factor, preferred_element_type=jnp.float32)
        combined = error_ref[block, :].astype(jnp.float32) - change_ref[block, :].astype(jnp.float32)
        error_out_ref[block, :] = (combined - approx).astype(jnp.bfloat16)
        copy = pltpu.make_async_copy(error_out_ref.at[block], error_hbm.at[block], sems.at[2 + k])
        copy.start()
        started.append(copy)
    approx = jnp.dot(basis_ref[pl.ds(rows, STATE), :], factor, preferred_element_type=jnp.float32)
    momentum = 0.9 * momentum_ref[...] + approx
    momentum_out_ref[...] = momentum
    update_ref[...] = (0.7 * (approx + 0.9 * momentum)).astype(jnp.bfloat16)
    for copy in (
        pltpu.make_async_copy(momentum_out_ref, momentum_hbm, sems.at[0]),
        pltpu.make_async_copy(update_ref, update_hbm, sems.at[1]),
    ):
        copy.start()
        started.append(copy)
    for copy in started:
        copy.wait()


def apply_factors(count, summed, inverse, basis, error, change, momentum):
    rows, columns = error.shape
    state = momentum.shape
    return pl.pallas_call(
        lambda *refs: apply_kernel(count, *refs),
        in_specs=[VMEM] * 6,
        out_specs=[HBM, HBM, HBM, VMEM],
        out_shape=[
            pltpu.HBM(state, jnp.bfloat16),
            pltpu.HBM(state, jnp.float32),
            pltpu.HBM((rows, columns), jnp.bfloat16),
            jax.ShapeDtypeStruct((RANK, columns), jnp.float32),
        ],
        scratch_shapes=[
            pltpu.VMEM(state, jnp.float32),
            pltpu.VMEM(state, jnp.bfloat16),
            pltpu.VMEM((rows, columns), jnp.bfloat16),
            pltpu.SemaphoreType.DMA((3 + rows // CHUNK,)),
        ],
        compiler_params=params(18),
        cost_estimate=pl.CostEstimate(
            flops=8 * RANK * rows * columns, bytes_accessed=6 * rows * columns, transcendentals=0
        ),
        name="apply",
    )(summed, inverse, basis, error, change, momentum)


def shards(inner_change, error_memory, momentum, q_prev):
    replicas = lax.axis_size("replica") // 2

    send, keep, error, change = left_factor(q_prev, error_memory, inner_change)
    own = keep + swap(send, ("c", 1))
    own = sum_four(own, "x", "y", (1, 3, 2), by_role=True)
    own = own + swap(own, ("z", 2), by_role=True)
    own = sum_four(own, "y", "x", (1, 3, 2), by_role=True)
    other = swap(own, ("c", 1))

    projected, whole, mine = right_factor(own, other, error, change)
    theirs = swap(mine, ("z", 1))
    summed = sum_four(projected, "y", "z", (3, 1, 2))
    summed, theirs = lax.optimization_barrier((summed, theirs))
    inverse, basis = make_basis(whole, mine, theirs)
    summed = sum_four(summed, "z", "y", (3, 1, 2))
    update, new_momentum, new_error, new_q = apply_factors(
        replicas, summed, inverse, basis, error, change, momentum
    )
    return (update, new_momentum, new_error, new_q)


def solution(mesh):
    in_specs = (
        P("replica", "tensor"),
        P("replica", "tensor"),
        P("replica", "tensor"),
        P(None, "tensor"),
    )
    out_specs = (
        P("replica", "tensor"),
        P("replica", "tensor"),
        P("replica", "tensor"),
        P(None, "tensor"),
    )
    return jax.shard_map(shards, mesh=mesh, in_specs=in_specs, out_specs=out_specs, check_vma=False)
```

```python
import jax
import jax.numpy as jnp
from jax import lax
from jax.experimental import pallas as pl
from jax.experimental.pallas import tpu as pltpu
from jax.sharding import PartitionSpec as P

RING = 4
BOTH = ("replica", "tensor")
RANK = 32
LEFT_CHUNK = 512
CHUNK = 256
STATE = 256
HBM = pl.BlockSpec(memory_space=pltpu.HBM)
VMEM = pl.BlockSpec(memory_space=pltpu.VMEM)


def role_of(x, y, core):
    return (core + x // 2 + y // 2) % 2


def pairs_of(specs, by_role):
    pairs = []
    for device in range(RING**3 * 2):
        core, x = device % 2, device // 2 % RING
        z, y = device // (2 * RING) % RING, device // (2 * RING * RING)
        kind = role_of(x, y, core) if by_role else core
        axis, flip = specs[kind]
        if axis == "c":
            core ^= flip
        else:
            x, y, z = x ^ (flip * (axis == "x")), y ^ (flip * (axis == "y")), z ^ (flip * (axis == "z"))
            if by_role:
                core = role_of(x, y, kind)
        pairs.append((device, ((y * RING + z) * RING + x) * 2 + core))
    return pairs


def swap(value, even, odd=None, by_role=False):
    return lax.ppermute(value, BOTH, pairs_of((even, odd or even), by_role))


def sum_four(value, even, odd, order, by_role=False):
    parts = {k: swap(value, (even, k), (odd, k), by_role) for k in order}
    return (value + parts[1]) + (parts[2] + parts[3])


def split(value, count):
    parts = []
    for _ in range(count):
        part = value.astype(jnp.bfloat16)
        parts.append(part)
        value = value - part.astype(jnp.float32)
    return parts


def fold(value):
    return (value[:RANK] + value[RANK : 2 * RANK]) + value[2 * RANK : 3 * RANK]


NT = (((1,), (1,)), ((), ()))


def params(mebibytes):
    return pltpu.CompilerParams(vmem_limit_bytes=mebibytes * 1024 * 1024)


def own_role():
    tensor, replica = lax.axis_index("tensor"), lax.axis_index("replica")
    return lax.rem(lax.rem(tensor, 2) + tensor // 4 + replica // 8, 2)


def left_terms(factor_ref, error_ref, change_ref, rows):
    term = jnp.dot(error_ref[rows, :], factor_ref[...], preferred_element_type=jnp.float32)
    term -= jnp.dot(change_ref[rows, :], factor_ref[...], preferred_element_type=jnp.float32)
    return fold(term.T)


def left_kernel(
    q_hbm, error_hbm, change_hbm, send_ref, keep_ref, factor_ref, error_ref, change_ref, q_ref, q_sem, sems
):
    role = own_role()
    half = send_ref.shape[1]
    count = 2 * half // LEFT_CHUNK
    fetch = pltpu.make_async_copy(q_hbm, q_ref, q_sem)
    fetch.start()
    blocks, copies = [], []
    for k in range(count):
        side = (1 - role) if k < count // 2 else role
        start = pl.multiple_of(side * half + k % (count // 2) * LEFT_CHUNK, LEFT_CHUNK)
        rows = pl.ds(start, LEFT_CHUNK)
        blocks.append(rows)
        copies.append([
            pltpu.make_async_copy(source.at[rows], target.at[rows], sems.at[j, k])
            for j, (source, target) in enumerate(((error_hbm, error_ref), (change_hbm, change_ref)))
        ])

    def begin(k):
        if k < count:
            for copy in copies[k]:
                copy.start()

    begin(0)
    fetch.wait()
    begin(1)
    parts = [part.astype(jnp.float32) for part in split(q_ref[...], 3)]
    stacked = jnp.concatenate(parts + [jnp.zeros_like(parts[0])], axis=0)
    factor_ref[...] = stacked.T.astype(jnp.bfloat16)
    for k in range(count):
        for copy in copies[k]:
            copy.wait()
        begin(k + 2)
        if k < count // 2:
            send_ref[:, k * LEFT_CHUNK : (k + 1) * LEFT_CHUNK] = left_terms(
                factor_ref, error_ref, change_ref, blocks[k]
            )
        elif k < count - 1:
            start = (k - count // 2) * LEFT_CHUNK
            keep_ref[:, start : start + LEFT_CHUNK] = left_terms(factor_ref, error_ref, change_ref, blocks[k])


def rest_kernel(factor_ref, error_ref, change_ref, keep_ref, out_ref):
    half = out_ref.shape[1]
    done = half - LEFT_CHUNK
    out_ref[:, :done] = keep_ref[...]
    rows = pl.ds(pl.multiple_of(own_role() * half + done, LEFT_CHUNK), LEFT_CHUNK)
    out_ref[:, done:] = left_terms(factor_ref, error_ref, change_ref, rows)


def left_factor(q_prev, error_memory, inner_change):
    rows, columns = error_memory.shape
    half = rows // 2
    send, keep, factor, error, change = pl.pallas_call(
        left_kernel,
        in_specs=[HBM, HBM, HBM],
        out_specs=[VMEM] * 5,
        out_shape=[
            pltpu.VMEM((RANK, half), jnp.float32),
            pltpu.VMEM((RANK, half - LEFT_CHUNK), jnp.float32),
            pltpu.VMEM((columns, 4 * RANK), jnp.bfloat16),
            pltpu.VMEM((rows, columns), jnp.bfloat16),
            pltpu.VMEM((rows, columns), jnp.bfloat16),
        ],
        scratch_shapes=[
            pltpu.VMEM((RANK, columns), jnp.float32),
            pltpu.SemaphoreType.DMA,
            pltpu.SemaphoreType.DMA((2, rows // LEFT_CHUNK)),
        ],
        compiler_params=params(8),
        cost_estimate=pl.CostEstimate(
            flops=12 * RANK * rows * columns, bytes_accessed=4 * rows * columns, transcendentals=0
        ),
        name="left_factor",
    )(*(pltpu.with_memory_space_constraint(value, pltpu.HBM) for value in (q_prev, error_memory, inner_change)))
    keep = pl.pallas_call(
        rest_kernel,
        in_specs=[VMEM] * 4,
        out_specs=VMEM,
        out_shape=pltpu.VMEM((RANK, half), jnp.float32),
        compiler_params=params(8),
        cost_estimate=pl.CostEstimate(
            flops=12 * RANK * LEFT_CHUNK * columns,
            bytes_accessed=4 * LEFT_CHUNK * columns,
            transcendentals=0,
        ),
        name="left_rest",
    )(factor, error, change, keep)
    return send, keep, error, change


def right_products(left_ref, error_ref, change_ref, side, previous_ref, out_ref):
    half, columns = left_ref.shape[1], error_ref.shape[1]
    rows = pl.ds(pl.multiple_of(side * half, half), half)
    factor = jnp.concatenate(split(left_ref[...], 3), axis=0)
    for start in range(0, columns, CHUNK):
        block = slice(start, start + CHUNK)
        term = jnp.dot(factor, error_ref[rows, block], preferred_element_type=jnp.float32)
        term -= jnp.dot(factor, change_ref[rows, block], preferred_element_type=jnp.float32)
        value = fold(term)
        if previous_ref is not None:
            value = value + previous_ref[:, block]
        out_ref[:, block] = value


def first_kernel(own_ref, error_ref, change_ref, out_ref):
    right_products(own_ref, error_ref, change_ref, own_role(), None, out_ref)


def second_kernel(other_ref, error_ref, change_ref, previous_ref, out_ref):
    right_products(other_ref, error_ref, change_ref, 1 - own_role(), previous_ref, out_ref)


def right_factor(own, other, error, change):
    rows, columns = error.shape
    half = own.shape[1]
    projected = None
    for kernel, left in ((first_kernel, own), (second_kernel, other)):
        more = [] if projected is None else [projected]
        projected = pl.pallas_call(
            kernel,
            in_specs=[VMEM] * (3 + len(more)),
            out_specs=VMEM,
            out_shape=pltpu.VMEM((RANK, columns), jnp.float32),
            compiler_params=params(8),
            cost_estimate=pl.CostEstimate(
                flops=12 * RANK * half * columns, bytes_accessed=4 * half * columns, transcendentals=0
            ),
            name="right_second" if more else "right_first",
        )(left, error, change, *more)
    return projected


def share_kernel(own_ref, other_ref, whole_ref, share_ref):
    role = own_role()
    half = own_ref.shape[1]
    whole_ref[:, pl.ds(pl.multiple_of(role * half, half), half)] = own_ref[...]
    whole_ref[:, pl.ds(pl.multiple_of((1 - role) * half, half), half)] = other_ref[...]
    factor = jnp.concatenate(split(whole_ref[...], 3), axis=0)
    squares = fold(lax.dot_general(factor, factor, NT, preferred_element_type=jnp.float32))
    gram = (squares[:, :RANK] + squares[:, RANK : 2 * RANK]) + squares[:, 2 * RANK :]
    share_ref[:, :128] = jnp.concatenate([gram, jnp.zeros((RANK, 128 - RANK), jnp.float32)], axis=1)
    position = lax.axis_index("replica")
    neighbour = position + 1 - 2 * lax.rem(position, 2)
    start = lax.rem(neighbour, 8) * STATE
    share_ref[:, 128:] = whole_ref[:, pl.ds(pl.multiple_of(start, STATE), STATE)]


def make_share(own, other):
    half = own.shape[1]
    return pl.pallas_call(
        share_kernel,
        in_specs=[VMEM] * 2,
        out_specs=[VMEM] * 2,
        out_shape=[
            pltpu.VMEM((RANK, 2 * half), jnp.float32),
            pltpu.VMEM((RANK, 128 + STATE), jnp.float32),
        ],
        compiler_params=params(8),
        cost_estimate=pl.CostEstimate(
            flops=36 * RANK * RANK * half, bytes_accessed=24 * RANK * half, transcendentals=0
        ),
        name="share",
    )(own, other)


def basis_kernel(whole_ref, mine_ref, theirs_ref, inverse_ref, basis_ref):
    width = 128
    row = lax.broadcasted_iota(jnp.int32, (RANK, width), 0)
    column = lax.broadcasted_iota(jnp.int32, (RANK, width), 1)
    gram = mine_ref[:, :width] + theirs_ref[:, :width]
    work = jnp.where(column < RANK, gram, jnp.where(column - RANK == row, 1.0, 0.0))
    for j in range(RANK):
        pivot = work[j : j + 1, :]
        scale = lax.rsqrt(pivot[:, j : j + 1])
        scaled = pivot * scale
        factor = work[:, j : j + 1] * scale
        work = jnp.where(row > j, work - factor * scaled, jnp.where(row == j, scaled, work))
    inverse = work[:, RANK : 2 * RANK]
    inverse_ref[...] = jnp.concatenate([inverse, jnp.zeros((RANK, width - RANK), jnp.float32)], axis=1)
    rows = whole_ref.shape[1]
    position = lax.axis_index("replica")
    start = lax.rem(position, 8) * STATE
    mine = whole_ref[:, pl.ds(pl.multiple_of(start, STATE), STATE)]
    state = jnp.where(lax.rem(position, 2) == position // 8, mine, theirs_ref[:, width:])
    for offset, count, value in ((0, rows, whole_ref[...]), (rows, STATE, state)):
        basis = jnp.dot(inverse, value, precision=lax.Precision.HIGHEST, preferred_element_type=jnp.float32)
        top, low = (part.astype(jnp.float32) for part in split(basis, 2))
        stacked = jnp.concatenate([top, low, top, low], axis=0)
        basis_ref[offset : offset + count, :] = stacked.T.astype(jnp.bfloat16)


def make_basis(whole, mine, theirs):
    rows = whole.shape[1]
    return pl.pallas_call(
        basis_kernel,
        in_specs=[VMEM] * 3,
        out_specs=[VMEM, VMEM],
        out_shape=[
            pltpu.VMEM((RANK, 128), jnp.float32),
            pltpu.VMEM((rows + STATE, 128), jnp.bfloat16),
        ],
        compiler_params=params(8),
        cost_estimate=pl.CostEstimate(
            flops=24 * RANK * RANK * rows, bytes_accessed=16 * RANK * rows, transcendentals=0
        ),
        name="basis",
    )(whole, mine, theirs)


def apply_kernel(
    count, summed_ref, inverse_ref, basis_ref, error_ref, change_ref, momentum_ref,
    update_hbm, momentum_hbm, error_hbm, q_ref,
    momentum_out_ref, update_ref, error_out_ref, sems,
):
    rows, columns = error_ref.shape
    new_q = (
        jnp.dot(
            inverse_ref[:, :RANK], summed_ref[...],
            precision=lax.Precision.HIGHEST, preferred_element_type=jnp.float32,
        )
        / count
    )
    q_ref[...] = new_q
    top, low = split(new_q, 2)
    factor = jnp.concatenate([top, top, low, low], axis=0)
    started = []
    starts = [0, CHUNK // 2, *range(CHUNK, rows, CHUNK), rows]
    for k, (start, end) in enumerate(zip(starts, starts[1:])):
        block = pl.ds(start, end - start)
        approx = jnp.dot(basis_ref[block, :], factor, preferred_element_type=jnp.float32)
        combined = error_ref[block, :].astype(jnp.float32) - change_ref[block, :].astype(jnp.float32)
        error_out_ref[block, :] = (combined - approx).astype(jnp.bfloat16)
        copy = pltpu.make_async_copy(error_out_ref.at[block], error_hbm.at[block], sems.at[2 + k])
        copy.start()
        started.append(copy)
    approx = jnp.dot(basis_ref[pl.ds(rows, STATE), :], factor, preferred_element_type=jnp.float32)
    momentum = 0.9 * momentum_ref[...] + approx
    momentum_out_ref[...] = momentum
    update_ref[...] = (0.7 * (approx + 0.9 * momentum)).astype(jnp.bfloat16)
    for copy in (
        pltpu.make_async_copy(momentum_out_ref, momentum_hbm, sems.at[0]),
        pltpu.make_async_copy(update_ref, update_hbm, sems.at[1]),
    ):
        copy.start()
        started.append(copy)
    for copy in started:
        copy.wait()


def apply_factors(count, summed, inverse, basis, error, change, momentum):
    rows, columns = error.shape
    state = momentum.shape
    return pl.pallas_call(
        lambda *refs: apply_kernel(count, *refs),
        in_specs=[VMEM] * 6,
        out_specs=[HBM, HBM, HBM, VMEM],
        out_shape=[
            pltpu.HBM(state, jnp.bfloat16),
            pltpu.HBM(state, jnp.float32),
            pltpu.HBM((rows, columns), jnp.bfloat16),
            jax.ShapeDtypeStruct((RANK, columns), jnp.float32),
        ],
        scratch_shapes=[
            pltpu.VMEM(state, jnp.float32),
            pltpu.VMEM(state, jnp.bfloat16),
            pltpu.VMEM((rows, columns), jnp.bfloat16),
            pltpu.SemaphoreType.DMA((3 + rows // CHUNK,)),
        ],
        compiler_params=params(18),
        cost_estimate=pl.CostEstimate(
            flops=8 * RANK * rows * columns, bytes_accessed=6 * rows * columns, transcendentals=0
        ),
        name="apply",
    )(summed, inverse, basis, error, change, momentum)


def shards(inner_change, error_memory, momentum, q_prev):
    replicas = lax.axis_size("replica") // 2

    send, keep, error, change = left_factor(q_prev, error_memory, inner_change)
    own = keep + swap(send, ("c", 1))
    own = sum_four(own, "x", "y", (1, 3, 2), by_role=True)
    own = own + swap(own, ("z", 2), by_role=True)
    own = sum_four(own, "y", "x", (1, 3, 2), by_role=True)
    other = swap(own, ("c", 1))

    projected = right_factor(own, other, error, change)
    whole, mine = make_share(own, other)
    theirs = swap(mine, ("z", 1))
    summed = sum_four(projected, "y", "z", (3, 1, 2))
    summed, theirs = lax.optimization_barrier((summed, theirs))
    inverse, basis = make_basis(whole, mine, theirs)
    summed = sum_four(summed, "z", "y", (3, 1, 2))
    update, new_momentum, new_error, new_q = apply_factors(
        replicas, summed, inverse, basis, error, change, momentum
    )
    return (update, new_momentum, new_error, new_q)


def solution(mesh):
    in_specs = (
        P("replica", "tensor"),
        P("replica", "tensor"),
        P("replica", "tensor"),
        P(None, "tensor"),
    )
    out_specs = (
        P("replica", "tensor"),
        P("replica", "tensor"),
        P("replica", "tensor"),
        P(None, "tensor"),
    )
    return jax.shard_map(shards, mesh=mesh, in_specs=in_specs, out_specs=out_specs, check_vma=False)
```

```python
import jax
import jax.numpy as jnp
from jax import lax
from jax.experimental import pallas as pl
from jax.experimental.pallas import tpu as pltpu
from jax.sharding import PartitionSpec as P

RING = 4
BOTH = ("replica", "tensor")
RANK = 32
LEFT_CHUNK = 512
CHUNK = 256
STATE = 256
HBM = pl.BlockSpec(memory_space=pltpu.HBM)
VMEM = pl.BlockSpec(memory_space=pltpu.VMEM)


def role_of(x, y, core):
    return (core + x // 2 + y // 2) % 2


def pairs_of(specs, by_role):
    pairs = []
    for device in range(RING**3 * 2):
        core, x = device % 2, device // 2 % RING
        z, y = device // (2 * RING) % RING, device // (2 * RING * RING)
        kind = role_of(x, y, core) if by_role else core
        axis, flip = specs[kind]
        if axis == "c":
            core ^= flip
        else:
            x, y, z = x ^ (flip * (axis == "x")), y ^ (flip * (axis == "y")), z ^ (flip * (axis == "z"))
            if by_role:
                core = role_of(x, y, kind)
        pairs.append((device, ((y * RING + z) * RING + x) * 2 + core))
    return pairs


def swap(value, even, odd=None, by_role=False):
    return lax.ppermute(value, BOTH, pairs_of((even, odd or even), by_role))


def sum_four(value, even, odd, order, by_role=False):
    parts = {k: swap(value, (even, k), (odd, k), by_role) for k in order}
    return (value + parts[1]) + (parts[2] + parts[3])


def split(value, count):
    parts = []
    for _ in range(count):
        part = value.astype(jnp.bfloat16)
        parts.append(part)
        value = value - part.astype(jnp.float32)
    return parts


def fold(value):
    return (value[:RANK] + value[RANK : 2 * RANK]) + value[2 * RANK : 3 * RANK]


NT = (((1,), (1,)), ((), ()))


def params(mebibytes):
    return pltpu.CompilerParams(vmem_limit_bytes=mebibytes * 1024 * 1024)


def own_role():
    tensor, replica = lax.axis_index("tensor"), lax.axis_index("replica")
    return lax.rem(lax.rem(tensor, 2) + tensor // 4 + replica // 8, 2)


def left_terms(factor_ref, error_ref, change_ref, rows):
    term = jnp.dot(error_ref[rows, :], factor_ref[...], preferred_element_type=jnp.float32)
    term -= jnp.dot(change_ref[rows, :], factor_ref[...], preferred_element_type=jnp.float32)
    return fold(term.T)


def left_kernel(
    q_hbm, error_hbm, change_hbm, send_ref, keep_ref, factor_ref, error_ref, change_ref, q_ref, q_sem, sems
):
    role = own_role()
    half = send_ref.shape[1]
    count = 2 * half // LEFT_CHUNK
    fetch = pltpu.make_async_copy(q_hbm, q_ref, q_sem)
    fetch.start()
    blocks, copies = [], []
    for k in range(count):
        side = (1 - role) if k < count // 2 else role
        start = pl.multiple_of(side * half + k % (count // 2) * LEFT_CHUNK, LEFT_CHUNK)
        rows = pl.ds(start, LEFT_CHUNK)
        blocks.append(rows)
        copies.append([
            pltpu.make_async_copy(source.at[rows], target.at[rows], sems.at[j, k])
            for j, (source, target) in enumerate(((error_hbm, error_ref), (change_hbm, change_ref)))
        ])

    def begin(k):
        if k < count:
            for copy in copies[k]:
                copy.start()

    begin(0)
    fetch.wait()
    begin(1)
    parts = [part.astype(jnp.float32) for part in split(q_ref[...], 3)]
    stacked = jnp.concatenate(parts + [jnp.zeros_like(parts[0])], axis=0)
    factor_ref[...] = stacked.T.astype(jnp.bfloat16)
    for k in range(count):
        for copy in copies[k]:
            copy.wait()
        begin(k + 2)
        if k < count // 2:
            send_ref[:, k * LEFT_CHUNK : (k + 1) * LEFT_CHUNK] = left_terms(
                factor_ref, error_ref, change_ref, blocks[k]
            )
        elif k < count - 1:
            start = (k - count // 2) * LEFT_CHUNK
            keep_ref[:, start : start + LEFT_CHUNK] = left_terms(factor_ref, error_ref, change_ref, blocks[k])


def rest_kernel(factor_ref, error_ref, change_ref, keep_ref, out_ref):
    half = out_ref.shape[1]
    done = half - LEFT_CHUNK
    out_ref[:, :done] = keep_ref[...]
    rows = pl.ds(pl.multiple_of(own_role() * half + done, LEFT_CHUNK), LEFT_CHUNK)
    out_ref[:, done:] = left_terms(factor_ref, error_ref, change_ref, rows)


def left_factor(q_prev, error_memory, inner_change):
    rows, columns = error_memory.shape
    half = rows // 2
    send, keep, factor, error, change = pl.pallas_call(
        left_kernel,
        in_specs=[HBM, HBM, HBM],
        out_specs=[VMEM] * 5,
        out_shape=[
            pltpu.VMEM((RANK, half), jnp.float32),
            pltpu.VMEM((RANK, half - LEFT_CHUNK), jnp.float32),
            pltpu.VMEM((columns, 4 * RANK), jnp.bfloat16),
            pltpu.VMEM((rows, columns), jnp.bfloat16),
            pltpu.VMEM((rows, columns), jnp.bfloat16),
        ],
        scratch_shapes=[
            pltpu.VMEM((RANK, columns), jnp.float32),
            pltpu.SemaphoreType.DMA,
            pltpu.SemaphoreType.DMA((2, rows // LEFT_CHUNK)),
        ],
        compiler_params=params(8),
        cost_estimate=pl.CostEstimate(
            flops=12 * RANK * rows * columns, bytes_accessed=4 * rows * columns, transcendentals=0
        ),
        name="left_factor",
    )(*(pltpu.with_memory_space_constraint(value, pltpu.HBM) for value in (q_prev, error_memory, inner_change)))
    keep = pl.pallas_call(
        rest_kernel,
        in_specs=[VMEM] * 4,
        out_specs=VMEM,
        out_shape=pltpu.VMEM((RANK, half), jnp.float32),
        compiler_params=params(8),
        cost_estimate=pl.CostEstimate(
            flops=12 * RANK * LEFT_CHUNK * columns,
            bytes_accessed=4 * LEFT_CHUNK * columns,
            transcendentals=0,
        ),
        name="left_rest",
    )(factor, error, change, keep)
    return send, keep, error, change


def right_products(left_ref, error_ref, change_ref, side, previous_ref, out_ref):
    half, columns = left_ref.shape[1], error_ref.shape[1]
    rows = pl.ds(pl.multiple_of(side * half, half), half)
    factor = jnp.concatenate(split(left_ref[...], 3), axis=0)
    for start in range(0, columns, CHUNK):
        block = slice(start, start + CHUNK)
        term = jnp.dot(factor, error_ref[rows, block], preferred_element_type=jnp.float32)
        term -= jnp.dot(factor, change_ref[rows, block], preferred_element_type=jnp.float32)
        value = fold(term)
        if previous_ref is not None:
            value = value + previous_ref[:, block]
        out_ref[:, block] = value


def first_kernel(own_ref, error_ref, change_ref, out_ref):
    right_products(own_ref, error_ref, change_ref, own_role(), None, out_ref)


def second_kernel(other_ref, error_ref, change_ref, previous_ref, out_ref):
    right_products(other_ref, error_ref, change_ref, 1 - own_role(), previous_ref, out_ref)


def right_factor(own, other, error, change):
    rows, columns = error.shape
    half = own.shape[1]
    projected = None
    for kernel, left in ((first_kernel, own), (second_kernel, other)):
        more = [] if projected is None else [projected]
        projected = pl.pallas_call(
            kernel,
            in_specs=[VMEM] * (3 + len(more)),
            out_specs=VMEM,
            out_shape=pltpu.VMEM((RANK, columns), jnp.float32),
            compiler_params=params(8),
            cost_estimate=pl.CostEstimate(
                flops=12 * RANK * half * columns, bytes_accessed=4 * half * columns, transcendentals=0
            ),
            name="right_second" if more else "right_first",
        )(left, error, change, *more)
    return projected


def share_kernel(own_ref, other_ref, whole_ref, share_ref):
    role = own_role()
    half = own_ref.shape[1]
    whole_ref[:, pl.ds(pl.multiple_of(role * half, half), half)] = own_ref[...]
    whole_ref[:, pl.ds(pl.multiple_of((1 - role) * half, half), half)] = other_ref[...]
    factor = jnp.concatenate(split(whole_ref[...], 3), axis=0)
    squares = fold(lax.dot_general(factor, factor, NT, preferred_element_type=jnp.float32))
    gram = (squares[:, :RANK] + squares[:, RANK : 2 * RANK]) + squares[:, 2 * RANK :]
    share_ref[:, :128] = jnp.concatenate([gram, jnp.zeros((RANK, 128 - RANK), jnp.float32)], axis=1)
    position = lax.axis_index("replica")
    neighbour = position + 1 - 2 * lax.rem(position, 2)
    start = lax.rem(neighbour, 8) * STATE
    share_ref[:, 128:] = whole_ref[:, pl.ds(pl.multiple_of(start, STATE), STATE)]


def make_share(own, other):
    half = own.shape[1]
    return pl.pallas_call(
        share_kernel,
        in_specs=[VMEM] * 2,
        out_specs=[VMEM] * 2,
        out_shape=[
            pltpu.VMEM((RANK, 2 * half), jnp.float32),
            pltpu.VMEM((RANK, 128 + STATE), jnp.float32),
        ],
        compiler_params=params(8),
        cost_estimate=pl.CostEstimate(
            flops=36 * RANK * RANK * half, bytes_accessed=24 * RANK * half, transcendentals=0
        ),
        name="share",
    )(own, other)


def basis_kernel(whole_ref, mine_ref, theirs_ref, inverse_ref, basis_ref):
    width = 128
    row = lax.broadcasted_iota(jnp.int32, (RANK, width), 0)
    column = lax.broadcasted_iota(jnp.int32, (RANK, width), 1)
    gram = mine_ref[:, :width] + theirs_ref[:, :width]
    work = jnp.where(column < RANK, gram, jnp.where(column - RANK == row, 1.0, 0.0))
    for j in range(RANK):
        pivot = work[j : j + 1, :]
        scale = lax.rsqrt(pivot[:, j : j + 1])
        scaled = pivot * scale
        factor = work[:, j : j + 1] * scale
        work = jnp.where(row > j, work - factor * scaled, jnp.where(row == j, scaled, work))
    inverse = work[:, RANK : 2 * RANK]
    one, two, three = split(inverse, 3)
    inverse_ref[...] = jnp.concatenate([one, two, three, one, two, one, *[jnp.zeros_like(one)] * 2], axis=1)
    rows = whole_ref.shape[1]
    position = lax.axis_index("replica")
    start = lax.rem(position, 8) * STATE
    mine = whole_ref[:, pl.ds(pl.multiple_of(start, STATE), STATE)]
    state = jnp.where(lax.rem(position, 2) == position // 8, mine, theirs_ref[:, width:])
    for offset, count, value in ((0, rows, whole_ref[...]), (rows, STATE, state)):
        basis = jnp.dot(inverse, value, precision=lax.Precision.HIGHEST, preferred_element_type=jnp.float32)
        top, low = (part.astype(jnp.float32) for part in split(basis, 2))
        stacked = jnp.concatenate([top, low, top, low], axis=0)
        basis_ref[offset : offset + count, :] = stacked.T.astype(jnp.bfloat16)


def make_basis(whole, mine, theirs):
    rows = whole.shape[1]
    return pl.pallas_call(
        basis_kernel,
        in_specs=[VMEM] * 3,
        out_specs=[VMEM, VMEM],
        out_shape=[
            pltpu.VMEM((RANK, 8 * RANK), jnp.bfloat16),
            pltpu.VMEM((rows + STATE, 128), jnp.bfloat16),
        ],
        compiler_params=params(8),
        cost_estimate=pl.CostEstimate(
            flops=24 * RANK * RANK * rows, bytes_accessed=16 * RANK * rows, transcendentals=0
        ),
        name="basis",
    )(whole, mine, theirs)


def apply_kernel(
    count, summed_ref, inverse_ref, basis_ref, error_ref, change_ref, momentum_ref,
    update_hbm, momentum_hbm, error_hbm, q_ref,
    momentum_out_ref, update_ref, error_out_ref, sems,
):
    rows, columns = error_ref.shape
    one, two, three = split(summed_ref[...], 3)
    stacked = jnp.concatenate([one, one, one, two, two, three], axis=0)
    new_q = jnp.dot(inverse_ref[:, : 6 * RANK], stacked, preferred_element_type=jnp.float32) / count
    q_ref[...] = new_q
    top, low = split(new_q, 2)
    factor = jnp.concatenate([top, top, low, low], axis=0)
    started = []
    starts = [0, CHUNK // 2, *range(CHUNK, rows, CHUNK), rows]
    for k, (start, end) in enumerate(zip(starts, starts[1:])):
        block = pl.ds(start, end - start)
        approx = jnp.dot(basis_ref[block, :], factor, preferred_element_type=jnp.float32)
        combined = error_ref[block, :].astype(jnp.float32) - change_ref[block, :].astype(jnp.float32)
        error_out_ref[block, :] = (combined - approx).astype(jnp.bfloat16)
        copy = pltpu.make_async_copy(error_out_ref.at[block], error_hbm.at[block], sems.at[2 + k])
        copy.start()
        started.append(copy)
    approx = jnp.dot(basis_ref[pl.ds(rows, STATE), :], factor, preferred_element_type=jnp.float32)
    momentum = 0.9 * momentum_ref[...] + approx
    momentum_out_ref[...] = momentum
    update_ref[...] = (0.7 * (approx + 0.9 * momentum)).astype(jnp.bfloat16)
    for copy in (
        pltpu.make_async_copy(momentum_out_ref, momentum_hbm, sems.at[0]),
        pltpu.make_async_copy(update_ref, update_hbm, sems.at[1]),
    ):
        copy.start()
        started.append(copy)
    for copy in started:
        copy.wait()


def apply_factors(count, summed, inverse, basis, error, change, momentum):
    rows, columns = error.shape
    state = momentum.shape
    return pl.pallas_call(
        lambda *refs: apply_kernel(count, *refs),
        in_specs=[VMEM] * 6,
        out_specs=[HBM, HBM, HBM, VMEM],
        out_shape=[
            pltpu.HBM(state, jnp.bfloat16),
            pltpu.HBM(state, jnp.float32),
            pltpu.HBM((rows, columns), jnp.bfloat16),
            jax.ShapeDtypeStruct((RANK, columns), jnp.float32),
        ],
        scratch_shapes=[
            pltpu.VMEM(state, jnp.float32),
            pltpu.VMEM(state, jnp.bfloat16),
            pltpu.VMEM((rows, columns), jnp.bfloat16),
            pltpu.SemaphoreType.DMA((3 + rows // CHUNK,)),
        ],
        compiler_params=params(18),
        cost_estimate=pl.CostEstimate(
            flops=8 * RANK * rows * columns, bytes_accessed=6 * rows * columns, transcendentals=0
        ),
        name="apply",
    )(summed, inverse, basis, error, change, momentum)


def shards(inner_change, error_memory, momentum, q_prev):
    replicas = lax.axis_size("replica") // 2

    send, keep, error, change = left_factor(q_prev, error_memory, inner_change)
    own = keep + swap(send, ("c", 1))
    own = sum_four(own, "x", "y", (1, 3, 2), by_role=True)
    own = own + swap(own, ("z", 2), by_role=True)
    own = sum_four(own, "y", "x", (1, 3, 2), by_role=True)
    other = swap(own, ("c", 1))

    projected = right_factor(own, other, error, change)
    whole, mine = make_share(own, other)
    theirs = swap(mine, ("z", 1))
    summed = sum_four(projected, "y", "z", (3, 1, 2))
    summed, theirs = lax.optimization_barrier((summed, theirs))
    inverse, basis = make_basis(whole, mine, theirs)
    summed = sum_four(summed, "z", "y", (3, 1, 2))
    update, new_momentum, new_error, new_q = apply_factors(
        replicas, summed, inverse, basis, error, change, momentum
    )
    return (update, new_momentum, new_error, new_q)


def solution(mesh):
    in_specs = (
        P("replica", "tensor"),
        P("replica", "tensor"),
        P("replica", "tensor"),
        P(None, "tensor"),
    )
    out_specs = (
        P("replica", "tensor"),
        P("replica", "tensor"),
        P("replica", "tensor"),
        P(None, "tensor"),
    )
    return jax.shard_map(shards, mesh=mesh, in_specs=in_specs, out_specs=out_specs, check_vma=False)
```
